32 devices in a mesh: grp: 2 (over x), row: 8 (over z, y), case: 2 (over core).
Axes of the slice: x: 2, y: 2, z: 4, core: 2. Of those that a mesh axis runs over, the one named last changes fastest.
Arguments:
- snapshots: float32 [4, 512, 4096], P(('grp', 'case'), 'row'), parts along dimension 0
- counts: int32 [4], P(('grp', 'case')), parts along dimension 0, may hold values from 256 to 512, as said below
- sketch: float32 [2, 512, 128], P('case'), may hold values from -6 to 6
- start_block: float32 [256, 128], replicated, may hold values from -6 to 6
Outputs:
- case_bases: float32 [4, 128, 4096], P(('grp', 'case'), None, 'row'), parts along dimension 0
- merged: float32 [256, 4096], P('grp', ('row', 'case')), parts along dimension 0
The draws below stay inside these ranges and needn't reach their ends.
There are 2 independent parts, one for each index of `grp`. The reference program is written for one: setup_inputs(seed, part) draws one part's arguments, and reference() takes and returns one part's arrays. A program takes and returns all parts, laid end to end along the dimension named above; an argument that names none is the same for every part. Nothing has to cross between parts.
Inputs may be any that keep to these rules, and one draw needn't show every extreme that they name: `counts`: one case of each part has all 512 snapshots valid; the valid snapshots of a case come first.
All inputs are finite; a program needn't handle non-finite values.
Results may differ from the reference program's by a relative error of at most 0.0003.
Values sent between devices are 32-bit elements; how exact they have to be, the bound alone decides.
No kernel may reach another device: no remote copies, remote signals or barrier semaphores. Data moves between devices by JAX's collectives and lax.ppermute only.
A program may use at most 128 MiB of HBM per device.

```python
import math
import jax
import jax.numpy as jnp
from jax import lax

S = 512
R = 128
ITERS = 2
EDGES = 4096
CASES = 2


def draw_snapshots(key, part):
    key = jax.random.fold_in(key, 11)
    key_noise, key_rows, key_cols = jax.random.split(key, 3)
    noise = jax.random.normal(key_noise, (CASES, S, EDGES), jnp.float32)
    row_scale = jnp.exp(jax.random.uniform(key_rows, (1, 1, EDGES), jnp.float32, 0.0, math.log(10.0)))
    col_scale = jnp.exp(jax.random.uniform(key_cols, (CASES, S, 1), jnp.float32, 0.0, math.log(3.0)))
    return (noise * col_scale * row_scale).astype(jnp.float32)


def draw_counts(key, part):
    key = jax.random.fold_in(key, 23)
    key_pick, key_values = jax.random.split(key, 2)
    chosen = jax.random.randint(key_pick, (), 0, CASES)
    values = jax.random.randint(key_values, (CASES,), S // 2, S + 1)
    return jnp.where(jnp.arange(CASES) == chosen, S, values).astype(jnp.int32)


def steps_of(rng, shape, shards, least, top_value):
    loudness, own = 1.0, jax.random.fold_in(rng, 6)
    for dim, blocks in shards:
        steps = jnp.exp(jax.random.uniform(jax.random.fold_in(own, dim), (blocks,), jnp.float32, least / len(shards), top_value / len(shards)))
        loudness = loudness * jnp.repeat(steps, shape[dim] // blocks).reshape([-1 if axis == dim else 1 for axis in range(len(shape))])
    return loudness


def scatter_about(own_key, dims, scale, bound, cuts=(), held_as=jnp.bfloat16):
    gain = steps_of(own_key, dims, cuts, -0.22, 0.18) if cuts else 1.0
    values = jax.random.normal(own_key, dims, jnp.float32) * scale * gain
    return jnp.minimum(jnp.maximum(values, -bound), bound).astype(held_as)


def setup_inputs(seed: int = 0, part: int = 0) -> dict:
    seeds = jax.random.split(jax.random.key(seed), 5)
    part_keys = jax.random.split(jax.random.fold_in(seeds[4], part), 5)
    return {
        "snapshots": draw_snapshots(jax.random.fold_in(jax.random.fold_in(seeds[4], part), 71), part),
        "counts": draw_counts(jax.random.fold_in(jax.random.fold_in(seeds[4], part), 71), part),
        "sketch": scatter_about(seeds[2], (CASES, S, R), 1.0, 6.0, ((0, 2),), jnp.float32),
        "start_block": scatter_about(seeds[3], (2 * R, R), 1.0, 6.0, (), jnp.float32),
    }


def lower_solve(factor, matrix):
    return jax.scipy.linalg.solve_triangular(factor, matrix, lower=True)

def reference(snapshots, counts, sketch, start_block):
    precise = lax.Precision.HIGHEST
    positions = jnp.arange(S, dtype=jnp.int32)
    scale_out = math.sqrt(EDGES)
    powered_list = []
    basis_list = []
    for case_index in range(CASES):
        valid_mask = (positions < counts[case_index]).astype(jnp.float32)
        active = snapshots[case_index] * valid_mask[:, None]
        sketch_rows = jnp.dot(sketch[case_index].T, active, precision=precise)
        gram_one = jnp.dot(sketch_rows, sketch_rows.T, precision=precise)
        ortho_one = lower_solve(jnp.linalg.cholesky(gram_one), sketch_rows)
        projected = jnp.dot(active, ortho_one.T, precision=precise)
        powered = jnp.dot(projected.T, active, precision=precise) / EDGES
        gram_two = jnp.dot(powered, powered.T, precision=precise)
        case_q = lower_solve(jnp.linalg.cholesky(gram_two), powered)
        powered_list.append(powered)
        basis_list.append(case_q * scale_out)
    stacked = jnp.concatenate(powered_list, axis=0)
    kernel = jnp.dot(stacked, stacked.T, precision=precise)
    vectors = start_block
    for sweep_index in range(ITERS):
        vectors = jnp.dot(kernel, vectors, precision=precise)
        chol_v = jnp.linalg.cholesky(jnp.dot(vectors.T, vectors, precision=precise))
        vectors = lower_solve(chol_v, vectors.T).T
    reduced = jnp.dot(vectors.T, jnp.dot(kernel, vectors, precision=precise), precision=precise)
    chol_m = jnp.linalg.cholesky(reduced)
    merged = lower_solve(chol_m, jnp.dot(vectors.T, stacked, precision=precise)) * scale_out
    return (jnp.stack(basis_list, axis=0), merged)
```

```python
import functools
import math

import jax
import jax.numpy as jnp
from jax import lax
from jax.experimental import pallas as pl
from jax.experimental.pallas import tpu as pltpu
from jax.sharding import PartitionSpec as P

ITERS = 2
TILE = 8
VMEM_BYTES = 32 * 1024 * 1024
precise = lax.Precision.HIGHEST


def dot(a, b, contract=(1, 0)):
    dims = (((contract[0],), (contract[1],)), ((), ()))
    return lax.dot_general(a, b, dims, precision=precise, preferred_element_type=jnp.float32)


def row_copies(value, row):
    return jnp.broadcast_to(value[row : row + 1, :], value.shape)


def inverse_cholesky(mats):
    size = mats[0].shape[0]
    tiles = size // TILE
    lane = lax.broadcasted_iota(jnp.int32, (TILE, size), 1)
    sublane = lax.broadcasted_iota(jnp.int32, (TILE, size), 0)
    stacks = [[m[TILE * i : TILE * (i + 1), :] for i in range(tiles)] for m in mats]
    for t in range(tiles):
        first = TILE * t
        in_panel = (lane >= first) & (lane < first + TILE)
        eye = (lane - first == sublane).astype(jnp.float32)
        for rows in stacks:
            column = lambda i, c: jnp.broadcast_to(rows[i][:, first + c : first + c + 1], (TILE, size))
            diag = [column(t, c) for c in range(TILE)]
            full = jnp.where(in_panel, eye, rows[t])
            factor = full
            for j in range(TILE):
                pivot = row_copies(diag[j], j)
                inverse = 1.0 / pivot
                here = sublane == j
                line = row_copies(full, j)
                factor = jnp.where(here, line * lax.rsqrt(pivot), factor)
                line = line * inverse
                full = jnp.where(here, line, full - diag[j] * line)
                for c in range(j + 1, TILE):
                    entry = row_copies(diag[c], j) * inverse
                    diag[c] = jnp.where(here, entry, diag[c] - diag[j] * entry)
            lines = [row_copies(full, c) for c in range(TILE)]
            for i in range(t + 1, tiles):
                total = jnp.where(in_panel, 0.0, rows[i])
                for c in range(TILE):
                    total = total - column(i, c) * lines[c]
                rows[i] = total
            rows[t] = factor
    lower = lax.broadcasted_iota(jnp.int32, (size, size), 1) <= lax.broadcasted_iota(jnp.int32, (size, size), 0)
    return [jnp.where(lower, jnp.concatenate(rows, axis=0), 0.0) for rows in stacks]


def call(kernel, out_shape, *args, smem=(), scratch=(), name=None, memory=pltpu.VMEM, grid_spec=None):
    specs = [pl.BlockSpec(memory_space=pltpu.SMEM if i in smem else memory) for i in range(len(args))]
    outs = jax.tree.map(lambda _: pl.BlockSpec(memory_space=memory), out_shape)
    return pl.pallas_call(
        kernel,
        out_shape=out_shape,
        in_specs=specs,
        out_specs=outs,
        scratch_shapes=scratch,
        compiler_params=pltpu.CompilerParams(vmem_limit_bytes=VMEM_BYTES),
        name=name,
    )(*args)


def f32(*shape):
    return jax.ShapeDtypeStruct(shape, jnp.float32)


def split_kernel(order, snapshots, *rest):
    outs, sems = rest[:-1], rest[-1]
    edges = outs[0].shape[-1]
    copies = []
    for k, out in enumerate(outs):
        chunk = order(k)
        columns = pl.ds(pl.multiple_of(chunk * edges, edges), edges)
        copies.append(pltpu.make_async_copy(snapshots.at[0, :, columns], out, sems.at[k]))
    for copy in copies:
        copy.start()
    for copy in copies:
        copy.wait()


def transposed_snapshots(snapshots, n):
    _, steps, edges = snapshots.shape
    edges = edges // n
    pairwise = n <= 8 and n & (n - 1) == 0
    if pairwise:
        order = lambda k: lax.axis_index("row") ^ k
    else:
        order = lambda k: k
    blocks = call(
        functools.partial(split_kernel, order),
        [f32(steps, edges)] * n,
        snapshots,
        scratch=[pltpu.SemaphoreType.DMA((n,))],
        memory=pl.ANY,
        name="split_edges",
    )
    if pairwise:
        got = [blocks[0]]
        for k in range(1, n):
            got.append(lax.ppermute(blocks[k], "row", [(i, i ^ k) for i in range(n)]))
        return got, order
    got = lax.all_to_all(jnp.stack(blocks), "row", 0, 0)
    return [got[k] for k in range(n)], order


def sketch_kernel(order, counts, sketch, *rest):
    blocks, active, product = rest[:-2], rest[-2], rest[-1]
    steps, edges = blocks[0].shape
    for k, block in enumerate(blocks):
        first = pl.multiple_of(order(k) * steps, steps)
        position = first + lax.broadcasted_iota(jnp.int32, (steps, edges), 0)
        valid = (position < counts[0]).astype(jnp.float32)
        active[pl.ds(first, steps), :] = block[...] * valid
    sketch_rows = dot(sketch[0], active[...], (0, 0))
    product[...] = dot(active[...], sketch_rows, (1, 1)).reshape(product.shape)


def powered_kernel(edge_count, sketch, product, active, powered):
    products = product[...].reshape(active.shape[0], -1)
    gram = dot(sketch[0], products, (0, 0))
    raw = dot(products, active[...], (0, 0))
    (inverse,) = inverse_cholesky([gram])
    powered[...] = dot(inverse, raw) / edge_count


def kernel_blocks_kernel(own, partner, out):
    rank = own.shape[0]
    half = rank // 2
    me = lax.axis_index("case")
    out[:rank, :] = dot(own[...], own[...], (1, 1))

    @pl.when(me == 0)
    def _():
        out[rank:, :] = dot(partner[:half, :], own[...], (1, 1))

    @pl.when(me == 1)
    def _():
        out[rank:, :] = dot(own[half:, :], partner[...], (1, 1))


def merge_kernel(scale_out, own_sums, partner_sums, own, partner, start, case_out, merged):
    rank = own.shape[0]
    first = lax.axis_index("case") == 0
    sums = jnp.where(first, own_sums[...], partner_sums[...]), jnp.where(first, partner_sums[...], own_sums[...])
    cross = jnp.concatenate([sums[0][rank:], sums[1][rank:]], axis=0)
    kernel = jnp.concatenate(
        [
            jnp.concatenate([sums[0][:rank], cross.T], axis=1),
            jnp.concatenate([cross, sums[1][:rank]], axis=1),
        ],
        axis=0,
    )
    vectors = start[...]
    for sweep_index in range(ITERS):
        vectors = dot(kernel, vectors)
        gram = dot(vectors, vectors, (0, 0))
        if sweep_index == 0:
            inverse, case_inverse = inverse_cholesky([gram, own_sums[:rank, :]])
            case_out[0] = dot(case_inverse, own[...]) * scale_out
        else:
            (inverse,) = inverse_cholesky([gram])
        vectors = dot(vectors, inverse, (1, 1))
    reduced = dot(vectors, dot(kernel, vectors), (0, 0))
    (inverse,) = inverse_cholesky([reduced])
    half = merged.shape[1]

    def project(columns):
        low = jnp.where(first, own[:, columns], partner[:, columns])
        high = jnp.where(first, partner[:, columns], own[:, columns])
        return dot(vectors, jnp.concatenate([low, high], axis=0), (0, 0))

    columns = pl.ds(pl.multiple_of(lax.axis_index("case") * half, half), half)
    merged[...] = dot(inverse, project(columns)) * scale_out


def sum_over_row(value, n):
    if n & (n - 1):
        return lax.psum(value, "row")
    apart = 1
    while apart < n:
        value = value + lax.ppermute(value, "row", [(i, i ^ apart) for i in range(n)])
        apart *= 2
    return value


def swapped(value):
    return lax.ppermute(value, "case", [(0, 1), (1, 0)])


def local(snapshots, counts, sketch, start_block):
    n = lax.axis_size("row")
    blocks, order = transposed_snapshots(snapshots, n)
    steps, edges = blocks[0].shape
    rank = sketch.shape[-1]
    edge_count = n * edges
    scale_out = math.sqrt(edge_count)
    active, product = call(
        functools.partial(sketch_kernel, order),
        [f32(n * steps, edges), f32(n, steps, rank)],
        counts,
        sketch,
        *blocks,
        smem=(0,),
        name="sketch_product",
    )
    part = jnp.sum(lax.all_to_all(product, "row", 0, 0), axis=0)
    product = lax.all_to_all(jnp.broadcast_to(part[None], (n, steps, rank)), "row", 0, 0)
    powered = call(
        functools.partial(powered_kernel, float(edge_count)), f32(rank, edges), sketch, product, active, name="powered"
    )
    partner = swapped(powered)
    sums = call(kernel_blocks_kernel, f32(rank + rank // 2, rank), powered, partner, name="kernel_blocks")
    sums = sum_over_row(sums, n)
    partner_sums = swapped(sums)
    case_out, merged = call(
        functools.partial(merge_kernel, scale_out),
        [f32(1, rank, edges), f32(rank, edges // 2)],
        sums,
        partner_sums,
        powered,
        partner,
        start_block,
        name="merge",
    )
    return case_out, merged


def solution(mesh):
    in_specs = (P(("grp", "case"), "row", None), P(("grp", "case")), P("case", None, None), P())
    out_specs = (P(("grp", "case"), None, "row"), P("grp", ("row", "case")))
    return jax.shard_map(local, mesh=mesh, in_specs=in_specs, out_specs=out_specs, check_vma=False)
```
